256 devices in a mesh: seq: 16 (over z_hi, y), head: 4 (over x), store: 4 (over z_lo, core).
Axes of the slice: x: 4, y: 4, z: 8 (z_hi: 4, z_lo: 2; z = z_hi * 2 + z_lo), core: 2. Of those that a mesh axis runs over, the one named last changes fastest.
Arguments:
- queries: bfloat16 [2048, 4096], P('seq', 'head'), may hold values from -160 to 160
- new_keys: bfloat16 [2048, 512], P('seq', 'head'), may hold values from -8 to 8
- new_values: bfloat16 [2048, 512], P('seq', 'head'), may hold values from -6 to 6
- pool_keys: bfloat16 [192, 256, 512], P(('seq', 'store'), None, 'head'), may hold values from -6 to 6
- pool_values: bfloat16 [192, 256, 512], P(('seq', 'store'), None, 'head'), may hold values from -6 to 6
- block_counts: int32 [64], P(('seq', 'store')), may hold values from 0 to 3, as said below
- out_weight: bfloat16 [4096, 8192], P(('head', 'store'), 'seq'), may hold values from -0.75 to 0.75
- residual: bfloat16 [2048, 8192], P('seq'), may hold values from -48 to 48
- ffn_gain: bfloat16 [8192], replicated, may hold values from 0.25 to 1.75
- gating_matrix: bfloat16 [8192, 14336], P('head', ('seq', 'store')), may hold values from -0.0625 to 0.0625
- up_weight: bfloat16 [8192, 14336], P('head', ('seq', 'store')), may hold values from -0.0625 to 0.0625
Outputs:
- gated: float32 [2048, 14336], P('head', ('seq', 'store'))
The draws below stay inside these ranges and needn't reach their ends.
Inputs may be any that keep to these rules, and one draw needn't show every extreme that they name: Holder g keeps its live blocks in its first block_counts[g] slots; some holder has all 3 slots live.
All inputs are finite; a program needn't handle non-finite values.
Results may differ from the reference program's by a relative error of at most 0.015.
Values may be sent and summed in bfloat16 or wider, within the bound.
A program may use at most 64 MiB of HBM per device.

```python
import math
import jax
import jax.numpy as jnp
from jax import lax

D = 8192
HD = 128
KVH = 4
GQ = 8
QH = 32
FF = 14336
BLK = 256
PLACES_EACH = 3
NEW_DEV = 128
NEW = 2048
STORE_HOLDERS = 64
POOL = 192
PIECE = 8
N_SEQ = 16
N_HEAD = 4
N_STORE = 4


def key_table(key):
    return jax.random.truncated_normal(key, -6.0, 6.0, (NEW, KVH * HD), jnp.float32)


def draw_new_keys(key, part):
    leading_displacement = key_table(key)
    return leading_displacement.astype(jnp.bfloat16)


def draw_queries(key, part):
    key = jax.random.fold_in(key, 7)
    values = 2.5 * jax.random.truncated_normal(key, -6.0, 6.0, (NEW, KVH * GQ * HD), jnp.float32)
    return values.astype(jnp.bfloat16)


def draw_block_counts(key, part):
    key = jax.random.fold_in(key, 11)
    key_start_offset, lookup_extent_lines, key_complete = jax.random.split(key, 3)
    leading_displacement = jax.random.randint(key_start_offset, (STORE_HOLDERS,), 0, PLACES_EACH + 1)
    transfer_extent = jax.random.randint(lookup_extent_lines, (STORE_HOLDERS,), 0, 8) == 0
    tally_sequence = jnp.where(transfer_extent, PLACES_EACH, leading_displacement)
    full_holder = jax.random.randint(key_complete, (), 0, STORE_HOLDERS)
    tally_sequence = jnp.where(jnp.arange(STORE_HOLDERS, dtype=jnp.int32) == full_holder, PLACES_EACH, tally_sequence)
    return tally_sequence.astype(jnp.int32)


def draw_residual(key, part):
    key = jax.random.fold_in(key, 13)
    key_noise, key_rows, key_cols = jax.random.split(key, 3)
    noise = jax.random.truncated_normal(key_noise, -4.0, 4.0, (NEW, D), jnp.float32)
    row_scale = jnp.exp(jax.random.uniform(key_rows, (NEW, 1), jnp.float32, jnp.log(0.2), jnp.log(2.0)))
    rising = jnp.exp(jnp.log(3.0) * jnp.arange(D, dtype=jnp.float32) / D)
    col_scale = rising * jnp.exp(jax.random.uniform(key_cols, (D,), jnp.float32, jnp.log(0.5), jnp.log(2.0)))
    return (noise * row_scale * col_scale[None, :]).astype(jnp.bfloat16)


def block_levels(own_key, extent, cuts, smallest, high):
    gain = 1.0
    for dim, parts in cuts:
        steps = jax.random.uniform(jax.random.fold_in(jax.random.fold_in(own_key, 6), dim), (parts,), jnp.float32, smallest / len(cuts), high / len(cuts))
        gain = gain * jnp.repeat(jnp.exp(steps), extent[dim] // parts).reshape((-1,) + (1,) * (len(extent) - 1 - dim))
    return gain


def bell_draw(rng, dims, deviation, reach, cuts=(), kind=jnp.bfloat16):
    result = jax.random.normal(rng, dims, jnp.float32) * deviation
    if len(cuts) > 0:
        result = block_levels(rng, dims, cuts, -0.22, 0.18) * result
    return jnp.clip(result, min=-reach, max=reach).astype(kind)


def setup_inputs(seed: int = 0) -> dict:
    seeds = jax.random.split(jax.random.key(seed), 12)
    queries = draw_queries(jax.random.fold_in(seeds[11], 71), 0)
    new_keys = draw_new_keys(jax.random.fold_in(seeds[11], 71), 0)
    new_values = bell_draw(seeds[2], (NEW, KVH * HD), 1.0, 6.0, ((0, 16), (1, 4)))
    pool_keys = bell_draw(seeds[3], (POOL, BLK, KVH * HD), 1.0, 6.0, ((0, 64), (2, 4)))
    pool_values = bell_draw(seeds[4], (POOL, BLK, KVH * HD), 1.0, 6.0, ((0, 64), (2, 4)))
    block_counts = draw_block_counts(jax.random.fold_in(seeds[11], 71), 0)
    out_weight = bell_draw(seeds[6], (QH * HD, D), (QH * HD // 64) ** -0.5, 0.75, ((0, 16), (1, 16)))
    residual = draw_residual(jax.random.fold_in(seeds[11], 71), 0)
    ffn_gain = jnp.clip(1.0 + 0.15 * jax.random.normal(seeds[8], (D,), jnp.float32), 0.25, 1.75).astype(jnp.bfloat16)
    gating_matrix = bell_draw(seeds[9], (D, FF), D ** -0.5, 0.0625, ((0, 4), (1, 64)))
    up_weight = bell_draw(seeds[10], (D, FF), D ** -0.5, 0.0625, ((0, 4), (1, 64)))
    return {"queries": queries, "new_keys": new_keys, "new_values": new_values, "pool_keys": pool_keys, "pool_values": pool_values, "block_counts": block_counts, "out_weight": out_weight, "residual": residual, "ffn_gain": ffn_gain, "gating_matrix": gating_matrix, "up_weight": up_weight}


neg_large = -1e+30
norm_eps = 1e-05

def reference(queries, new_keys, new_values, pool_keys, pool_values, block_counts, out_weight, residual, ffn_gain, gating_matrix, up_weight):
    slot_index = jnp.arange(POOL, dtype=jnp.int32)
    slot_live = slot_index % PLACES_EACH < block_counts[slot_index // PLACES_EACH]
    key_live = jnp.repeat(slot_live, BLK)
    cached_keys = pool_keys.reshape(POOL * BLK, KVH, HD)
    cached_values = pool_values.reshape(POOL * BLK, KVH, HD)
    fresh_keys = new_keys.reshape(NEW, KVH, HD)
    fresh_values = new_values.reshape(NEW, KVH, HD)
    query_heads = queries.reshape(NEW, KVH, GQ, HD)
    token_index = jnp.arange(NEW, dtype=jnp.int32)
    score_scale = 1.0 / math.sqrt(HD)
    rows_block = NEW_DEV * GQ

    def head_context(head_index):
        keys_all = jnp.concatenate([lax.dynamic_index_in_dim(cached_keys, head_index, 1, keepdims=False), lax.dynamic_index_in_dim(fresh_keys, head_index, 1, keepdims=False)], axis=0)
        entire_payloads = jnp.concatenate([lax.dynamic_index_in_dim(cached_values, head_index, 1, keepdims=False), lax.dynamic_index_in_dim(fresh_values, head_index, 1, keepdims=False)], axis=0)
        queries_head = lax.dynamic_index_in_dim(query_heads, head_index, 1, keepdims=False)

        def block_context(block_index):
            first_row = block_index * NEW_DEV
            query_rows = lax.dynamic_slice_in_dim(queries_head, first_row, NEW_DEV, 0).reshape(rows_block, HD)
            scores = jnp.dot(query_rows, keys_all.T, preferred_element_type=jnp.float32) * score_scale
            row_token = first_row + jnp.arange(rows_block, dtype=jnp.int32) // GQ
            visible = jnp.concatenate([jnp.broadcast_to(key_live[None, :], (rows_block, POOL * BLK)), token_index[None, :] <= row_token[:, None]], axis=1)
            masked = jnp.where(visible, scores, neg_large)
            row_max = lax.optimization_barrier(jnp.max(masked, axis=1, keepdims=True))
            weights = jnp.where(visible, jnp.exp(masked - row_max), 0.0)
            context = jnp.dot(weights.astype(jnp.bfloat16), entire_payloads, preferred_element_type=jnp.float32) / lax.optimization_barrier(jnp.sum(weights, axis=1, keepdims=True))
            return context.reshape(NEW_DEV, GQ * HD)
        return lax.map(block_context, jnp.arange(N_SEQ, dtype=jnp.int32)).reshape(NEW, GQ * HD)
    per_head = lax.map(head_context, jnp.arange(KVH, dtype=jnp.int32))
    context = jnp.transpose(per_head, (1, 0, 2)).reshape(NEW, KVH * GQ * HD).astype(jnp.bfloat16)
    attention_out = jnp.dot(context, out_weight, preferred_element_type=jnp.float32)
    attended = (residual.astype(jnp.float32) + attention_out).astype(jnp.bfloat16)
    attended_wide = attended.astype(jnp.float32)
    inv_rms = lax.rsqrt(lax.optimization_barrier(jnp.mean(attended_wide * attended_wide, axis=1)) + norm_eps)
    scaled = (attended_wide * ffn_gain.astype(jnp.float32)[None, :]).astype(jnp.bfloat16)
    gate_value = jnp.dot(scaled, gating_matrix, preferred_element_type=jnp.float32) * inv_rms[:, None]
    up_value = jnp.dot(scaled, up_weight, preferred_element_type=jnp.float32) * inv_rms[:, None]
    gated = jax.nn.silu(gate_value) * up_value
    gated = gated.reshape(N_SEQ, N_HEAD, N_STORE, PIECE, FF).transpose(1, 0, 2, 3, 4).reshape(NEW, FF)
    return gated
```

```python
import math

import jax
import jax.numpy as jnp
from jax import lax
from jax.experimental import pallas as pl
from jax.experimental.pallas import tpu as pltpu
from jax.sharding import Mesh, PartitionSpec as P

axes = ("zh", "y", "x", "zl", "c")
sizes = (4, 4, 4, 2, 2)
neg_large = -1e30
pos_large = 1e30
norm_eps = 1e-05
head_dim = 128
score_log2 = math.log2(math.e) / math.sqrt(head_dim)
MESH = pl.DeviceIdType.MESH
nt = (((1,), (1,)), ((), ()))


class Copies:
    def __init__(self, send, recv):
        self.send, self.recv, self.count, self.started = send, recv, 0, []

    def make(self, src, dst, where):
        at = self.count
        self.count += 1
        return pltpu.make_async_remote_copy(
            src_ref=src,
            dst_ref=dst,
            send_sem=self.send.at[at],
            recv_sem=self.recv.at[at],
            device_id=where,
            device_id_type=MESH,
        )

    def go(self, src, dst, where):
        copy = self.make(src, dst, where)
        copy.start()
        self.started.append(copy)
        return copy

    def finish(self):
        for copy in self.started:
            copy.wait_send()


class Locals:
    def __init__(self, sems):
        self.sems, self.count = sems, 0

    def go(self, src, dst):
        copy = pltpu.make_async_copy(src, dst, self.sems.at[self.count])
        self.count += 1
        copy.start()
        return copy


def position():
    return tuple(lax.axis_index(name) for name in axes)


def around(index, extent, step):
    return lax.rem(index + (step + extent), extent)


def greet(peers):
    barrier = pltpu.get_barrier_semaphore()
    for where in peers:
        pl.semaphore_signal(barrier, inc=1, device_id=where, device_id_type=MESH)
    pl.semaphore_wait(barrier, len(peers))


def gather_kernel(
    keys, values, new_keys, new_values, queries, counts,
    keys_out, values_out, new_keys_out, new_values_out, queries_out, counts_out,
    send, recv, local,
):
    zh, y, x, zl, c = position()
    other = 1 - c
    right, left, far = around(y, 4, 1), around(y, 4, -1), around(y, 4, 2)
    up, down, top = around(zh, 4, 1), around(zh, 4, -1), around(zh, 4, 2)
    lane_peers = [{"y": around(y, 4, step), "c": core} for step in (1, 3, 2) for core in (c, other)]
    lane_peers.append({"c": other})
    greet(lane_peers + [{"zh": up}, {"zh": down}])
    copies, here = Copies(send, recv), Locals(local)
    half = keys.shape[0] // 2

    def first(src, dst):
        return copies.go(src, dst, {"y": right}), copies.go(src, dst, {"y": left})

    ring_k = first(keys, keys_out.at[y, c])
    ring_v = first(values, values_out.at[y, c])
    ring_q = []
    for part in range(2):
        src = queries.at[:, pl.ds(pl.multiple_of(part * 512 + c * 256, 256), 256)]
        ring_q.append(
            (
                copies.go(src, queries_out.at[zh, part], {"zh": up}),
                copies.go(src, queries_out.at[zh, part], {"zh": down}),
            )
        )
    tallies = [copies.go(counts, counts_out.at[y, c], where) for where in lane_peers]
    ring_nk = first(new_keys, new_keys_out.at[y])
    ring_nv = first(new_values, new_values_out.at[y])
    across = [
        copies.go(keys, keys_out.at[y, c], {"c": other}),
        copies.go(values, values_out.at[y, c], {"c": other}),
    ]
    own = [
        here.go(keys, keys_out.at[y, c]),
        here.go(values, values_out.at[y, c]),
        here.go(new_keys, new_keys_out.at[y]),
        here.go(new_values, new_values_out.at[y]),
        here.go(counts, counts_out.at[y, c]),
    ]
    for part in range(2):
        src = queries.at[:, pl.ds(pl.multiple_of(part * 512 + c * 256, 256), 256)]
        own.append(here.go(src, queries_out.at[zh, part]))

    onward = []
    for ring, out in ((ring_k, keys_out), (ring_v, values_out)):
        ring[0].wait_recv()
        piece = out.at[left, c, pl.ds(0, half)]
        one = copies.go(piece, piece, {"y": right})
        ring[1].wait_recv()
        piece = out.at[right, c, pl.ds(half, half)]
        two = copies.go(piece, piece, {"y": left})
        for side in (left, right):
            whole = out.at[side, c]
            across.append(copies.go(whole, whole, {"c": other}))
        onward.append((one, two, out))
    final = []
    for ring, out in ((ring_nk, new_keys_out), (ring_nv, new_values_out)):
        ring[0].wait_recv()
        piece = out.at[left, pl.ds(0, 64)]
        final.append(copies.go(piece, piece, {"y": right}))
        ring[1].wait_recv()
        piece = out.at[right, pl.ds(64, 64)]
        final.append(copies.go(piece, piece, {"y": left}))
    ring_q[0][0].wait_recv()
    piece = queries_out.at[down, 0]
    final.append(copies.go(piece, piece, {"zh": up}))
    ring_q[1][1].wait_recv()
    piece = queries_out.at[up, 1]
    final.append(copies.go(piece, piece, {"zh": down}))
    ring_q[0][1].wait_recv()
    ring_q[1][0].wait_recv()
    for one, two, out in onward:
        one.wait_recv()
        piece = out.at[far, c, pl.ds(0, half)]
        across.append(copies.go(piece, piece, {"c": other}))
        two.wait_recv()
        piece = out.at[far, c, pl.ds(half, half)]
        across.append(copies.go(piece, piece, {"c": other}))
    for copy in tallies + final + across:
        copy.wait_recv()
    for copy in own:
        copy.wait()
    copies.finish()


def attention_kernel(
    counts, queries, keys, values, new_keys, new_values, out, stats,
    live, query_rows, top, total, weighted,
):
    zq = pl.program_id(0)
    zh, y, x, zl, c = position()
    rows = query_rows.shape[0]
    step_rows = 256

    @pl.when(zq == 0)
    def _():
        found = jnp.int32(0)
        for holder in range(8):
            tally = counts[holder // 2, holder % 2, 0, 0]
            for slot in range(3):
                live[found] = holder * 3 + slot
                found = found + (slot < tally).astype(jnp.int32)
        live[found] = 0
        live[31] = found

    for part in range(2):
        for head in range(2):
            query_rows[pl.ds((part * 2 + head) * 128, 128), :] = queries[
                0, part, :, pl.ds(head * 128, 128)
            ]
    top[...] = jnp.full(top.shape, neg_large, jnp.float32)
    total[...] = jnp.zeros(total.shape, jnp.float32)
    weighted[...] = jnp.zeros(weighted.shape, jnp.float32)

    def wide(value):
        return jnp.concatenate([value, value], axis=1)

    @pl.when(zq >= zh)
    def _():
        keys_now = jnp.concatenate([new_keys[2 * zl], new_keys[2 * zl + 1]], axis=0)
        values_now = jnp.concatenate([new_values[2 * zl], new_values[2 * zl + 1]], axis=0)
        key_token = (zh * 4 + 2 * zl) * 128 + lax.broadcasted_iota(jnp.int32, (128, 256), 1)
        query_token = (zq * 4 + y) * 128 + lax.broadcasted_iota(jnp.int32, (128, 256), 0)
        visible = key_token <= query_token
        for first in range(0, rows, 128):
            at = pl.ds(first, 128)
            scores = lax.dot_general(
                query_rows[at, :], keys_now, nt, preferred_element_type=jnp.float32
            )
            scores = jnp.where(visible, scores, neg_large)
            top_now = jnp.broadcast_to(jnp.max(scores, axis=1, keepdims=True), (128, 128))
            weights = jnp.where(visible, jnp.exp2((scores - wide(top_now)) * score_log2), 0.0)
            top[at, :] = top_now
            total[at, :] = weights[:, :128] + weights[:, 128:]
            weighted[at, :] = jnp.dot(
                weights.astype(jnp.bfloat16), values_now, preferred_element_type=jnp.float32
            )

    found = live[31]

    def turn(step, carry):
        one, two = live[2 * step], live[2 * step + 1]
        both = 2 * step + 1 < found
        for first in range(0, rows, step_rows):
            at = pl.ds(first, step_rows)
            rows_now = query_rows[at, :]
            scores_one = lax.dot_general(
                rows_now, keys[one], nt, preferred_element_type=jnp.float32
            )
            scores_two = lax.dot_general(
                rows_now, keys[two], nt, preferred_element_type=jnp.float32
            )
            top_one = jnp.maximum(scores_one[:, :128], scores_one[:, 128:])
            top_two = jnp.maximum(scores_two[:, :128], scores_two[:, 128:])
            best = jnp.maximum(top_one, jnp.where(both, top_two, neg_large))
            old = top[at, :]
            new = jnp.maximum(old, jnp.max(best, axis=1, keepdims=True))
            factor = jnp.exp2((old - new) * score_log2)
            shift_two = jnp.where(both, new, pos_large)
            weights_one = jnp.exp2((scores_one - wide(new)) * score_log2)
            weights_two = jnp.exp2((scores_two - wide(shift_two)) * score_log2)
            top[at, :] = new
            total[at, :] = total[at, :] * factor + (
                (weights_one[:, :128] + weights_one[:, 128:])
                + (weights_two[:, :128] + weights_two[:, 128:])
            )
            weighted[at, :] = (
                weighted[at, :] * factor
                + jnp.dot(
                    weights_one.astype(jnp.bfloat16),
                    values[one],
                    preferred_element_type=jnp.float32,
                )
                + jnp.dot(
                    weights_two.astype(jnp.bfloat16),
                    values[two],
                    preferred_element_type=jnp.float32,
                )
            )
        return carry

    lax.fori_loop(0, (found + 1) // 2, turn, 0)
    for part in range(2):
        at = pl.ds(part * 256, 256)
        sums = jnp.broadcast_to(jnp.sum(total[at, :], axis=1, keepdims=True), (256, 128))
        out[0, part] = (weighted[at, :] / jnp.where(sums > 0.0, sums, 1.0)).astype(jnp.bfloat16)
        tops = jnp.transpose(top[at, :])[:8]
        sums = jnp.transpose(sums)[:8]
        line = lax.broadcasted_iota(jnp.int32, (8, 256), 0)
        stats[0, part] = jnp.where(line < 4, tops, sums)


def project_kernel(
    parts, stats, out_weight, residual, attended,
    parts_in, stats_in, context, weight, rest, partial, sibling, joined, x_in, x_sum, z_in, z_out,
    send, recv, local,
):
    zh, y, x, zl, c = position()
    other = 1 - c
    right, left, far = around(y, 4, 1), around(y, 4, -1), around(y, 4, 2)
    east, west, beyond = around(x, 4, 1), around(x, 4, -1), around(x, 4, 2)
    z = 2 * zh + zl
    column = []
    for step in (4, 3, 5, 2, 6, 1, 7):
        there = around(z, 8, step)
        column.append((there // 2, lax.rem(there, 2)))
    greet(
        [{"zh": a, "zl": b} for a, b in column]
        + [{"y": right}, {"y": left}, {"y": far}]
        + [{"x": east}, {"x": west}, {"c": other}]
    )
    copies, here = Copies(send, recv), Locals(local)
    arriving = []
    for a, b in column:
        arriving.append(copies.go(stats.at[a, b], stats_in.at[z], {"zh": a, "zl": b}))
        arriving.append(copies.go(parts.at[a, b], parts_in.at[z], {"zh": a, "zl": b}))
    group = pl.ds(pl.multiple_of((2 * zl + c) * 32, 32), 32)

    def tile(to):
        return residual.at[group, pl.ds(pl.multiple_of(x * 2048 + to * 512, 512), 512)]

    rest_in = [copies.go(tile(to), rest.at[y], {"y": to}) for to in (right, left, far)]
    own = [
        here.go(stats.at[zh, zl], stats_in.at[z]),
        here.go(parts.at[zh, zl], parts_in.at[z]),
        here.go(out_weight, weight),
        here.go(tile(y), rest.at[y]),
    ]
    for copy in arriving:
        copy.wait_recv()
    for copy in own:
        copy.wait()
    tops = jnp.concatenate([stats_in[i, pl.ds(0, 1), :] for i in range(8)], axis=0)
    sums = jnp.concatenate([stats_in[i, pl.ds(4, 1), :] for i in range(8)], axis=0)
    scales = jnp.exp2((tops - jnp.max(tops, axis=0, keepdims=True)) * score_log2) * sums
    scales = scales / jnp.sum(scales, axis=0, keepdims=True)
    scales = jnp.transpose(
        jnp.concatenate([scales, jnp.zeros((120, 256), jnp.float32)], axis=0)
    )
    for head in range(2):
        at = pl.ds(head * 128, 128)
        acc = jnp.zeros((128, 128), jnp.float32)
        for i in range(8):
            acc += parts_in[i, at, :].astype(jnp.float32) * scales[
                head * 128 : (head + 1) * 128, i : i + 1
            ]
        context[y, :, at] = acc.astype(jnp.bfloat16)
    to_right = copies.go(context.at[y], context.at[y], {"y": right})
    to_left = copies.go(context.at[y], context.at[y], {"y": left})

    def project(source):
        for xd in range(4):
            product = jnp.dot(
                context[source], weight[xd], preferred_element_type=jnp.float32
            ).astype(jnp.bfloat16)
            for a in range(2):
                for b in range(2):
                    first = (2 * a + b) * 32
                    partial[b, source, xd, a] = product[first : first + 32]
        return copies.go(partial.at[other, source], sibling.at[source], {"c": other})

    order = [y, left, right, far]
    swaps = [project(y)]
    to_right.wait_recv()
    piece = context.at[left, pl.ds(0, 64)]
    on_right = copies.go(piece, piece, {"y": right})
    to_left.wait_recv()
    piece = context.at[right, pl.ds(64, 64)]
    on_left = copies.go(piece, piece, {"y": left})
    swaps.append(project(left))
    swaps.append(project(right))
    on_right.wait_recv()
    on_left.wait_recv()
    swaps.append(project(far))

    def add(one, two):
        return one.astype(jnp.float32) + two.astype(jnp.float32)

    hops = []
    for source, swap in zip(order, swaps):
        swap.wait_recv()
        for xd in (beyond, east, west, x):
            joined[source, xd] = add(partial[c, source, xd], sibling[source, xd]).astype(
                jnp.bfloat16
            )
        hops.append(
            (
                copies.go(joined.at[source, beyond, 0], x_in.at[source, 0], {"x": east}),
                copies.go(joined.at[source, beyond, 1], x_in.at[source, 1], {"x": west}),
            )
        )
    lasts = []
    for source, (by_east, by_west) in zip(order, hops):
        by_east.wait_recv()
        x_sum[source, 0, 0] = add(joined[source, east, 0], x_in[source, 0]).astype(jnp.bfloat16)
        x_sum[source, 0, 1] = joined[source, east, 1]
        one = copies.go(x_sum.at[source, 0], x_in.at[source, pl.ds(2, 2)], {"x": east})
        by_west.wait_recv()
        x_sum[source, 1, 0] = joined[source, west, 0]
        x_sum[source, 1, 1] = add(joined[source, west, 1], x_in[source, 1]).astype(jnp.bfloat16)
        two = copies.go(x_sum.at[source, 1], x_in.at[source, pl.ds(4, 2)], {"x": west})
        lasts.append((one, two))
    pairs = []
    for source, (one, two) in zip(order, lasts):
        one.wait_recv()
        two.wait_recv()
        away = 1 - zl
        z_out[source] = (
            add(joined[source, x, away], x_in[source, 2 + away])
            + x_in[source, 4 + away].astype(jnp.float32)
        ).astype(jnp.bfloat16)
        pairs.append(copies.go(z_out.at[source], z_in.at[source], {"zl": away}))
    for copy in rest_in:
        copy.wait_recv()
    for source, pair in zip(order, pairs):
        pair.wait_recv()
        summed = (
            add(joined[source, x, zl], x_in[source, 2 + zl])
            + x_in[source, 4 + zl].astype(jnp.float32)
            + z_in[source].astype(jnp.float32)
        )
        attended[source] = (rest[source].astype(jnp.float32) + summed).astype(jnp.bfloat16)
    copies.finish()


def feed_kernel(
    attended, gain, gating, up_weight, summed,
    tokens, weight, product, half_in, whole_in, send, recv, local,
):
    zh, y, x, zl, c = position()
    other = 1 - c
    right, left, far = around(y, 4, 1), around(y, 4, -1), around(y, 4, 2)
    east, west, beyond = around(x, 4, 1), around(x, 4, -1), around(x, 4, 2)
    z = 2 * zh + zl
    above, below = around(z, 8, 1), around(z, 8, -1)
    over = {"zh": above // 2, "zl": lax.rem(above, 2)}
    under = {"zh": below // 2, "zl": lax.rem(below, 2)}
    greet([over, under, {"y": right}, {"y": left}, {"x": east}, {"x": west}, {"c": other}])
    copies, here = Copies(send, recv), Locals(local)

    def piece(feature, plane, part, rows=64, first=0):
        return tokens.at[feature, plane, c, pl.ds(part * 64 + first, rows)]

    def move(ref, where):
        return copies.go(ref, ref, where)

    own = here.go(attended, tokens.at[y, z, c])
    loads = [
        here.go(gating, weight.at[pl.ds(0, 224)]),
        here.go(up_weight, weight.at[pl.ds(256, 224)]),
    ]
    weight[pl.ds(224, 32), :] = jnp.zeros((32, 2048), jnp.bfloat16)
    weight[pl.ds(480, 32), :] = jnp.zeros((32, 2048), jnp.bfloat16)
    own.wait()
    shared = []

    def share(ref):
        shared.append(move(ref, {"c": other}))

    a_over, a_under = move(piece(y, z, 0), over), move(piece(y, z, 0), under)
    b_right, b_left = move(piece(y, z, 1), {"y": right}), move(piece(y, z, 1), {"y": left})
    rows_y = [(z, move(piece(y, z, 0), {"y": right}), move(piece(y, z, 0), {"y": left}))]
    cols = {}

    def start_column(name, feature):
        cols[name] = [
            feature,
            move(piece(feature, z, 1), over),
            move(piece(feature, z, 1), under),
        ]

    start_column("own", y)
    share(tokens.at[y, z, c])

    def spread(plane):
        rows_y.append(
            (plane, move(piece(y, plane, 0), {"y": right}), move(piece(y, plane, 0), {"y": left}))
        )
        share(piece(y, plane, 0))

    halves = []

    def turn_row(index):
        plane, to_right, to_left = rows_y[index]
        to_right.wait_recv()
        one = move(piece(left, plane, 0, 32, 0), {"y": right})
        share(piece(left, plane, 0))
        to_left.wait_recv()
        two = move(piece(right, plane, 0, 32, 32), {"y": left})
        share(piece(right, plane, 0))
        halves.append((plane, one, two))

    def end_row(index):
        plane, one, two = halves[index]
        one.wait_recv()
        two.wait_recv()
        share(piece(far, plane, 0))

    def turn_column(name, step):
        feature, up_copy, down_copy = cols[name]
        up_copy.wait_recv()
        plane = around(z, 8, -step)
        if step < 4:
            cols[name][1] = move(piece(feature, plane, 1), over)
        share(piece(feature, plane, 1))
        if step < 4:
            down_copy.wait_recv()
            plane = around(z, 8, step)
            if step < 3:
                cols[name][2] = move(piece(feature, plane, 1), under)
            share(piece(feature, plane, 1))

    def turn_part0(step):
        nonlocal a_over, a_under
        a_over.wait_recv()
        plane = around(z, 8, -step)
        if step < 4:
            a_over = move(piece(y, plane, 0), over)
        spread(plane)
        if step < 4:
            a_under.wait_recv()
            plane = around(z, 8, step)
            if step < 3:
                a_under = move(piece(y, plane, 0), under)
            spread(plane)

    b_right.wait_recv()
    b_far_one = move(piece(left, z, 1, 32, 0), {"y": right})
    start_column("left", left)
    b_left.wait_recv()
    b_far_two = move(piece(right, z, 1, 32, 32), {"y": left})
    start_column("right", right)
    share(piece(left, z, 1))
    share(piece(right, z, 1))
    turn_part0(1)
    b_far_one.wait_recv()
    b_far_two.wait_recv()
    start_column("far", far)
    share(piece(far, z, 1))
    turn_column("own", 1)
    turn_part0(2)
    turn_row(0)
    turn_column("left", 1)
    turn_column("right", 1)
    turn_part0(3)
    turn_row(1)
    turn_row(2)
    turn_column("far", 1)
    turn_column("own", 2)
    turn_part0(4)
    end_row(0)
    turn_column("left", 2)
    turn_row(3)
    turn_column("right", 2)
    turn_row(4)
    end_row(1)
    end_row(2)
    turn_column("far", 2)
    turn_column("own", 3)
    turn_row(5)
    turn_row(6)
    end_row(3)
    turn_column("left", 3)
    turn_column("right", 3)
    turn_row(7)
    end_row(4)
    turn_column("far", 3)
    turn_column("own", 4)
    end_row(5)
    turn_column("left", 4)
    end_row(6)
    turn_column("right", 4)
    end_row(7)
    turn_column("far", 4)
    for copy in loads:
        copy.wait()
    for copy in shared:
        copy.wait_recv()

    lane = lax.broadcasted_iota(jnp.int32, (512, 512), 1)

    def multiply(group):
        line, core = group // 2, lax.rem(group, 2)
        acc = jnp.zeros((512, 512), jnp.float32)
        squares = jnp.zeros((512, 128), jnp.float32)
        for feature in range(4):
            block = jnp.concatenate(
                [tokens[feature, 2 * a + line, core] for a in range(4)], axis=0
            ).astype(jnp.float32)
            square = block * block
            squares += (square[:, :128] + square[:, 128:256]) + (
                square[:, 256:384] + square[:, 384:]
            )
            at = pl.ds(feature * 512, 512)
            scaled = (block * gain[:, at]).astype(jnp.bfloat16)
            acc += lax.dot_general(
                scaled, weight[:, at], nt, preferred_element_type=jnp.float32
            )
        squares = jnp.sum(squares, axis=1, keepdims=True)
        high = squares.astype(jnp.bfloat16).astype(jnp.float32)
        low = squares - high
        return jnp.where(lane == 224, high, jnp.where(lane == 225, low, acc))

    def add(one, two):
        return one.astype(jnp.float32) + two.astype(jnp.float32)

    product[0] = multiply(beyond).astype(jnp.bfloat16)
    one = copies.go(product.at[0, pl.ds(0, 256)], half_in.at[0], {"x": east})
    two = copies.go(product.at[0, pl.ds(256, 256)], half_in.at[1], {"x": west})
    block = multiply(east)
    one.wait_recv()
    product[1, pl.ds(0, 256)] = (block[:256] + half_in[0].astype(jnp.float32)).astype(jnp.bfloat16)
    product[1, pl.ds(256, 256)] = block[256:].astype(jnp.bfloat16)
    one = copies.go(product.at[1], whole_in.at[0], {"x": east})
    block = multiply(west)
    two.wait_recv()
    product[2, pl.ds(0, 256)] = block[:256].astype(jnp.bfloat16)
    product[2, pl.ds(256, 256)] = (block[256:] + half_in[1].astype(jnp.float32)).astype(
        jnp.bfloat16
    )
    two = copies.go(product.at[2], whole_in.at[1], {"x": west})
    block = multiply(x)
    one.wait_recv()
    two.wait_recv()
    summed[...] = block + add(whole_in[0], whole_in[1])
    copies.finish()


any_spec = pl.BlockSpec(memory_space=pl.ANY)
vmem_spec = pl.BlockSpec(memory_space=pltpu.VMEM)
bf16, f32 = jnp.bfloat16, jnp.float32
mib = 1024 * 1024


def gather(keys, values, new_keys, new_values, queries, counts):
    shapes = [
        ((4, 2, 768, 128), bf16),
        ((4, 2, 768, 128), bf16),
        ((4, 128, 128), bf16),
        ((4, 128, 128), bf16),
        ((4, 2, 128, 256), bf16),
        ((4, 2, 8, 128), jnp.int32),
    ]
    return pl.pallas_call(
        gather_kernel,
        out_shape=[jax.ShapeDtypeStruct(*shape) for shape in shapes],
        in_specs=[any_spec] * 6,
        out_specs=[any_spec] * 6,
        scratch_shapes=[
            pltpu.SemaphoreType.DMA((48,)),
            pltpu.SemaphoreType.DMA((48,)),
            pltpu.SemaphoreType.DMA((8,)),
        ],
        compiler_params=pltpu.CompilerParams(collective_id=1, has_side_effects=True),
        name="gather",
    )(keys, values, new_keys, new_values, queries, counts)


def attend(counts, queries, keys, values, new_keys, new_values):
    def whole(shape):
        return pl.BlockSpec(shape, lambda i: (0,) * len(shape))

    return pl.pallas_call(
        attention_kernel,
        grid=(4,),
        out_shape=[
            jax.ShapeDtypeStruct((4, 2, 256, 128), bf16),
            jax.ShapeDtypeStruct((4, 2, 8, 256), f32),
        ],
        in_specs=[
            pl.BlockSpec(memory_space=pltpu.SMEM),
            pl.BlockSpec((1, 2, 128, 256), lambda i: (i, 0, 0, 0)),
            whole((24, 256, 128)),
            whole((24, 256, 128)),
            whole((4, 128, 128)),
            whole((4, 128, 128)),
        ],
        out_specs=[
            pl.BlockSpec((1, 2, 256, 128), lambda i: (i, 0, 0, 0)),
            pl.BlockSpec((1, 2, 8, 256), lambda i: (i, 0, 0, 0)),
        ],
        scratch_shapes=[
            pltpu.SMEM((32,), jnp.int32),
            pltpu.VMEM((512, 128), bf16),
            pltpu.VMEM((512, 128), f32),
            pltpu.VMEM((512, 128), f32),
            pltpu.VMEM((512, 128), f32),
        ],
        compiler_params=pltpu.CompilerParams(vmem_limit_bytes=32 * mib),
        name="attend",
    )(counts, queries, keys, values, new_keys, new_values)


def project(parts, stats, out_weight, residual):
    return pl.pallas_call(
        project_kernel,
        out_shape=jax.ShapeDtypeStruct((4, 32, 512), bf16),
        in_specs=[any_spec] * 4,
        out_specs=vmem_spec,
        scratch_shapes=[
            pltpu.VMEM((8, 256, 128), bf16),
            pltpu.VMEM((8, 8, 256), f32),
            pltpu.VMEM((4, 128, 256), bf16),
            pltpu.VMEM((4, 256, 512), bf16),
            pltpu.VMEM((4, 32, 512), bf16),
            pltpu.VMEM((2, 4, 4, 2, 32, 512), bf16),
            pltpu.VMEM((4, 4, 2, 32, 512), bf16),
            pltpu.VMEM((4, 4, 2, 32, 512), bf16),
            pltpu.VMEM((4, 6, 32, 512), bf16),
            pltpu.VMEM((4, 2, 2, 32, 512), bf16),
            pltpu.VMEM((4, 32, 512), bf16),
            pltpu.VMEM((4, 32, 512), bf16),
            pltpu.SemaphoreType.DMA((64,)),
            pltpu.SemaphoreType.DMA((64,)),
            pltpu.SemaphoreType.DMA((8,)),
        ],
        compiler_params=pltpu.CompilerParams(
            collective_id=2, has_side_effects=True, vmem_limit_bytes=32 * mib
        ),
        name="project",
    )(parts, stats, out_weight, residual)


def feed(attended, gain, gating, up_weight):
    return pl.pallas_call(
        feed_kernel,
        out_shape=jax.ShapeDtypeStruct((512, 512), f32),
        in_specs=[any_spec, vmem_spec, any_spec, any_spec],
        out_specs=vmem_spec,
        scratch_shapes=[
            pltpu.VMEM((4, 8, 2, 128, 512), bf16),
            pltpu.VMEM((512, 2048), bf16),
            pltpu.VMEM((3, 512, 512), bf16),
            pltpu.VMEM((2, 256, 512), bf16),
            pltpu.VMEM((2, 512, 512), bf16),
            pltpu.SemaphoreType.DMA((160,)),
            pltpu.SemaphoreType.DMA((160,)),
            pltpu.SemaphoreType.DMA((8,)),
        ],
        compiler_params=pltpu.CompilerParams(
            collective_id=3, has_side_effects=True, vmem_limit_bytes=48 * mib
        ),
        name="feed",
    )(attended, gain, gating, up_weight)


def on_device(
    queries,
    new_keys,
    new_values,
    pool_keys,
    pool_values,
    block_counts,
    out_weight,
    residual,
    ffn_gain,
    gating_matrix,
    up_weight,
):
    weights = lax.all_gather(out_weight, "zh", axis=0)
    counts = jnp.broadcast_to(block_counts.reshape(1, 1), (8, 128))
    keys, values, all_new_keys, all_new_values, all_queries, all_counts = gather(
        pool_keys.reshape(768, 128),
        pool_values.reshape(768, 128),
        new_keys,
        new_values,
        queries,
        counts,
    )
    parts, stats = attend(
        all_counts,
        all_queries,
        keys.reshape(24, 256, 128),
        values.reshape(24, 256, 128),
        all_new_keys,
        all_new_values,
    )
    attended = project(parts, stats, weights, residual)
    x = lax.axis_index("x")
    gain = lax.dynamic_slice(ffn_gain, (x * 2048,), (2048,)).astype(f32).reshape(1, 2048)
    summed = feed(attended.reshape(128, 512), gain, gating_matrix.T, up_weight.T)
    squares = summed[:, 224] + summed[:, 225]
    inv_rms = lax.rsqrt(squares / 8192.0 + norm_eps)
    gate = summed[:, :224] * inv_rms[:, None]
    up = summed[:, 256:480] * inv_rms[:, None]
    return jax.nn.silu(gate) * up


def solution(mesh):
    fine = Mesh(mesh.devices.reshape(sizes), axes)
    seq, head, store = ("zh", "y"), "x", ("zl", "c")
    in_specs = (
        P(seq, head),
        P(seq, head),
        P(seq, head),
        P(seq + store, None, head),
        P(seq + store, None, head),
        P(seq + store),
        P((head,) + store, seq),
        P(seq, None),
        P(),
        P(head, seq + store),
        P(head, seq + store),
    )
    out_specs = P(head, seq + store)
    return jax.shard_map(
        on_device, mesh=fine, in_specs=in_specs, out_specs=out_specs, check_vma=False
    )
```

```python
import math

import jax
import jax.numpy as jnp
from jax import lax
from jax.experimental import pallas as pl
from jax.experimental.pallas import tpu as pltpu
from jax.sharding import Mesh, PartitionSpec as P

axes = ("zh", "y", "x", "zl", "c")
sizes = (4, 4, 4, 2, 2)
neg_large = -1e30
pos_large = 1e30
norm_eps = 1e-05
head_dim = 128
score_log2 = math.log2(math.e) / math.sqrt(head_dim)
MESH = pl.DeviceIdType.MESH
nt = (((1,), (1,)), ((), ()))


class Copies:
    def __init__(self, send, recv):
        self.send, self.recv, self.count, self.started = send, recv, 0, []

    def make(self, src, dst, where):
        at = self.count
        self.count += 1
        return pltpu.make_async_remote_copy(
            src_ref=src,
            dst_ref=dst,
            send_sem=self.send.at[at],
            recv_sem=self.recv.at[at],
            device_id=where,
            device_id_type=MESH,
        )

    def go(self, src, dst, where):
        copy = self.make(src, dst, where)
        copy.start()
        self.started.append(copy)
        return copy

    def finish(self):
        for copy in self.started:
            copy.wait_send()


class Locals:
    def __init__(self, sems):
        self.sems, self.count = sems, 0

    def go(self, src, dst):
        copy = pltpu.make_async_copy(src, dst, self.sems.at[self.count])
        self.count += 1
        copy.start()
        return copy


def position():
    return tuple(lax.axis_index(name) for name in axes)


def around(index, extent, step):
    return lax.rem(index + (step + extent), extent)


def greet(peers):
    barrier = pltpu.get_barrier_semaphore()
    for where in peers:
        pl.semaphore_signal(barrier, inc=1, device_id=where, device_id_type=MESH)
    pl.semaphore_wait(barrier, len(peers))


class Ring:
    def __init__(self, copies, index, extent, forward, backward, piece, arrived):
        self.copies, self.index, self.extent = copies, index, extent
        self.ways, self.piece, self.arrived = (forward, backward), piece, arrived
        self.pending = [self.move(index, way) for way in range(2)]
        self.step = 0

    def move(self, at, way, part=None):
        ref = self.piece(at, part)
        return self.copies.go(ref, ref, self.ways[way])

    def turn(self):
        self.step += 1
        step, last = self.step, self.extent // 2
        for way in range(2):
            self.pending[way].wait_recv()
            if step < last:
                at = around(self.index, self.extent, step if way else -step)
                part = way if step == last - 1 else None
                self.pending[way] = self.move(at, way, part)
                self.arrived(at)
        if step == last:
            self.arrived(around(self.index, self.extent, last))


def whole_kernel(
    keys, values, new_keys, new_values, queries, counts, out_weight, residual, gain, gating,
    up_weight, summed,
    keys_all, values_all, new_keys_all, new_values_all, queries_all, counts_all, top, total,
    weighted, parts, stats, parts_in, stats_in, context, project_weight, rest, partial, sibling,
    joined, x_in, x_sum, z_in, z_out, tokens, weight, product, half_in, whole_in,
    send, recv, local,
):
    zh, y, x, zl, c = position()
    other = 1 - c
    right, left, far = around(y, 4, 1), around(y, 4, -1), around(y, 4, 2)
    east, west, beyond = around(x, 4, 1), around(x, 4, -1), around(x, 4, 2)
    z = 2 * zh + zl
    above, below = around(z, 8, 1), around(z, 8, -1)
    over = {"zh": above // 2, "zl": lax.rem(above, 2)}
    under = {"zh": below // 2, "zl": lax.rem(below, 2)}
    column = []
    for step in (4, 3, 5, 2, 6, 1, 7):
        there = around(z, 8, step)
        column.append({"zh": there // 2, "zl": lax.rem(there, 2)})
    lane_peers = [{"y": around(y, 4, step), "c": core} for step in (1, 3, 2) for core in (c, other)]
    lane_peers.append({"c": other})
    greet(lane_peers + column + [{"x": east}, {"x": west}])
    copies, here = Copies(send, recv), Locals(local)

    up, down = around(zh, 4, 1), around(zh, 4, -1)
    half = keys.shape[0] // 2

    def first(src, dst):
        return copies.go(src, dst, {"y": right}), copies.go(src, dst, {"y": left})

    def head_pair(part):
        return queries.at[:, pl.ds(pl.multiple_of(part * 512 + c * 256, 256), 256)]

    fresh_in = []
    for src, out in ((new_keys, new_keys_all), (new_values, new_values_all)):
        for to in (far, right, left):
            fresh_in.append(copies.go(src, out.at[y], {"y": to}))
    across = {
        "k": copies.go(keys, keys_all.at[y, c], {"c": other}),
        "v": copies.go(values, values_all.at[y, c], {"c": other}),
    }
    ring_q = []
    for part in range(2):
        to = queries_all.at[zh, part]
        ring_q.append(
            (
                copies.go(head_pair(part), to, {"zh": up}),
                copies.go(head_pair(part), to, {"zh": down}),
            )
        )
    tallies = [copies.go(counts, counts_all.at[y, c], where) for where in lane_peers]
    ring_k = first(keys, keys_all.at[y, c])
    ring_v = first(values, values_all.at[y, c])
    own = [
        here.go(keys, keys_all.at[y, c]),
        here.go(values, values_all.at[y, c]),
        here.go(counts, counts_all.at[y, c]),
        here.go(head_pair(0), queries_all.at[zh, 0]),
        here.go(head_pair(1), queries_all.at[zh, 1]),
        here.go(new_keys, new_keys_all.at[y]),
        here.go(new_values, new_values_all.at[y]),
    ]
    group = pl.ds(pl.multiple_of((2 * zl + c) * 32, 32), 32)

    def tile(to):
        return residual.at[group, pl.ds(pl.multiple_of(x * 2048 + to * 512, 512), 512)]

    rest_in = [copies.go(tile(to), rest.at[y], {"y": to}) for to in (right, left, far)]
    own_late = [
        here.go(out_weight, project_weight.at[zh]),
        here.go(tile(y), rest.at[y]),
    ]
    loads = [
        here.go(gating, weight.at[pl.ds(0, 224)]),
        here.go(up_weight, weight.at[pl.ds(256, 224)]),
    ]
    weight[pl.ds(224, 32), :] = jnp.zeros((32, 2048), jnp.bfloat16)
    weight[pl.ds(480, 32), :] = jnp.zeros((32, 2048), jnp.bfloat16)

    def wide(value):
        return jnp.concatenate([value, value], axis=1)

    def meet(zq, part, holders, fresh=False, with_new=False):
        rows = jnp.concatenate(
            [queries_all[zq, part, :, pl.ds(0, 128)], queries_all[zq, part, :, pl.ds(128, 128)]],
            axis=0,
        )
        at = pl.ds(part * 256, 256)
        best, blocks = None, []
        for there, core in holders:
            scores = lax.dot_general(
                rows, keys_all[there, core], nt, preferred_element_type=jnp.float32
            )
            tally = counts_all[there, core]
            for slot in range(3):
                dead = jnp.where(tally > slot, -pos_large, pos_large).astype(jnp.float32)[:1]
                piece = scores[:, slot * 256 : (slot + 1) * 256]
                highest = jnp.minimum(jnp.maximum(piece[:, :128], piece[:, 128:]), -dead)
                best = highest if best is None else jnp.maximum(best, highest)
                blocks.append((piece, dead))
        if with_new:
            keys_now = jnp.concatenate(
                [new_keys_all[2 * zl], new_keys_all[2 * zl + 1]], axis=0
            )
            scores = lax.dot_general(rows, keys_now, nt, preferred_element_type=jnp.float32)
            key_token = (zh * 4 + 2 * zl) * 128 + lax.broadcasted_iota(jnp.int32, (256, 256), 1)
            query_token = (zq * 4 + y) * 128 + lax.rem(
                lax.broadcasted_iota(jnp.int32, (256, 256), 0), 128
            )
            scores = jnp.where(key_token <= query_token, scores, -pos_large)
            best = jnp.maximum(best, jnp.maximum(scores[:, :128], scores[:, 128:]))
            new_scores = jnp.where(key_token <= query_token, scores, -3.0 * pos_large)
        highest = jnp.max(best, axis=1, keepdims=True)
        if fresh:
            now = jnp.broadcast_to(highest, (256, 128))
        else:
            old = top[zq, at, :]
            now = jnp.maximum(old, highest)
            factor = jnp.exp2((old - now) * score_log2)
        top[zq, at, :] = now
        weights = [
            jnp.exp2((piece - wide(jnp.maximum(now, dead))) * score_log2) for piece, dead in blocks
        ]
        if with_new:
            weights.append(jnp.exp2((new_scores - wide(now)) * score_log2))
        sums = None
        for value in weights:
            added = value[:, :128] + value[:, 128:]
            sums = added if sums is None else sums + added
        if not fresh:
            sums = sums + total[zq, at, :] * factor
        total[zq, at, :] = sums
        acc = None if fresh else weighted[zq, at, :] * factor
        for number, (there, core) in enumerate(holders):
            three = jnp.concatenate(
                [value.astype(jnp.bfloat16) for value in weights[number * 3 : number * 3 + 3]],
                axis=1,
            )
            one = jnp.dot(three, values_all[there, core], preferred_element_type=jnp.float32)
            acc = one if acc is None else acc + one
        if with_new:
            values_now = jnp.concatenate(
                [new_values_all[2 * zl], new_values_all[2 * zl + 1]], axis=0
            )
            acc = acc + jnp.dot(
                weights[-1].astype(jnp.bfloat16), values_now, preferred_element_type=jnp.float32
            )
        weighted[zq, at, :] = acc

    both_own = [(y, c), (y, other)]
    both_sides = [(left, c), (right, c), (left, other), (right, other)]
    both_far = [(far, c), (far, other)]

    def near(zq):
        for part in range(2):
            meet(zq, part, both_own, fresh=True, with_new=True)

    def sides(zq):
        for part in range(2):
            meet(zq, part, both_sides)

    for copy in own:
        copy.wait()
    across["k"].wait_recv()
    across["v"].wait_recv()
    for copy in fresh_in + tallies[6:]:
        copy.wait_recv()
    near(zh)
    for pair_q in ring_q:
        for copy in pair_q:
            copy.wait_recv()
    far_q = [
        copies.go(queries_all.at[down, 0], queries_all.at[down, 0], {"zh": up}),
        copies.go(queries_all.at[up, 1], queries_all.at[up, 1], {"zh": down}),
    ]
    for copy in own_late:
        copy.wait()

    def weight_piece(at, part):
        if part is None:
            return project_weight.at[at]
        return project_weight.at[at, pl.ds(part * 128, 128)]

    ring_w = Ring(copies, zh, 4, {"zh": up}, {"zh": down}, weight_piece, lambda at: None)
    near(down)
    onward = []

    def pass_on(name, ring, out):
        ring[0].wait_recv()
        piece = out.at[left, c, pl.ds(0, half)]
        one = copies.go(piece, piece, {"y": right})
        across[name, 0] = copies.go(out.at[left, c], out.at[left, c], {"c": other})
        ring[1].wait_recv()
        piece = out.at[right, c, pl.ds(half, half)]
        two = copies.go(piece, piece, {"y": left})
        across[name, 1] = copies.go(out.at[right, c], out.at[right, c], {"c": other})
        onward.append((one, two, out))

    pass_on("k", ring_k, keys_all)
    near(up)
    pass_on("v", ring_v, values_all)
    for copy in far_q:
        copy.wait_recv()
    near(around(zh, 4, 2))
    for name in ("k", "v"):
        for side in range(2):
            across[name, side].wait_recv()
    for copy in tallies[:4]:
        copy.wait_recv()

    def turn(number, carry):
        sides(around(zh, 4, number))
        return carry

    lax.fori_loop(0, 2, turn, 0)
    for number, (one, two, out) in enumerate(onward):
        one.wait_recv()
        two.wait_recv()
        across["far", number] = copies.go(out.at[far, c], out.at[far, c], {"c": other})
    ring_w.turn()
    lax.fori_loop(2, 4, turn, 0)
    across["far", 0].wait_recv()
    across["far", 1].wait_recv()
    for copy in tallies[4:6]:
        copy.wait_recv()
    arriving = []
    for step in (2, 1, 3, 0):
        zq = around(zh, 4, step)
        for part in range(2):
            meet(zq, part, both_far)
            at = pl.ds(part * 256, 256)
            sums = jnp.broadcast_to(
                jnp.sum(total[zq, at, :], axis=1, keepdims=True), (256, 128)
            )
            parts[zq, part] = (weighted[zq, at, :] / jnp.where(sums > 0.0, sums, 1.0)).astype(
                jnp.bfloat16
            )
            lane = lax.broadcasted_iota(jnp.int32, (256, 128), 1)
            stats[zq, part] = jnp.transpose(jnp.where(lane < 4, top[zq, at, :], sums))[:8]
        for to in (zl, 1 - zl):
            if step == 0 and to is zl:
                continue
            where = {"zh": zq, "zl": to}
            arriving.append(copies.go(stats.at[zq, to], stats_in.at[z], where))
            arriving.append(copies.go(parts.at[zq, to], parts_in.at[z], where))
    stats_in[z] = stats[zh, zl]
    parts_in[z] = parts[zh, zl]
    ring_w.turn()
    for copy in arriving:
        copy.wait_recv()
    tops = jnp.concatenate([stats_in[i, pl.ds(0, 1), :] for i in range(8)], axis=0)
    sums = jnp.concatenate([stats_in[i, pl.ds(4, 1), :] for i in range(8)], axis=0)
    scales = jnp.exp2((tops - jnp.max(tops, axis=0, keepdims=True)) * score_log2) * sums
    scales = scales / jnp.sum(scales, axis=0, keepdims=True)
    scales = jnp.transpose(
        jnp.concatenate([scales, jnp.zeros((120, 256), jnp.float32)], axis=0)
    )
    for head in range(2):
        at = pl.ds(head * 128, 128)
        acc = jnp.zeros((128, 128), jnp.float32)
        for i in range(8):
            acc += parts_in[i, at, :].astype(jnp.float32) * scales[
                head * 128 : (head + 1) * 128, i : i + 1
            ]
        context[y, :, at] = acc.astype(jnp.bfloat16)

    context_in = [
        copies.go(context.at[y], context.at[y], {"y": to}) for to in (far, right, left)
    ]
    for copy in context_in:
        copy.wait_recv()
    for copy in rest_in:
        copy.wait_recv()

    def add(one, two):
        return one.astype(jnp.float32) + two.astype(jnp.float32)

    swaps, hops, lasts, pairs = {}, {}, {}, {}

    def project(k):
        for xd in range(4):
            block = jnp.dot(
                context[k], project_weight[xd], preferred_element_type=jnp.float32
            ).astype(jnp.bfloat16)
            for a in range(2):
                for b in range(2):
                    first = (2 * a + b) * 32
                    partial[b, k, xd, a] = block[first : first + 32]
        swaps[k] = copies.go(partial.at[other, k], sibling.at[k], {"c": other})

    def hop(k):
        swaps[k].wait_recv()
        for xd in (beyond, east, west, x):
            joined[k, xd] = add(partial[c, k, xd], sibling[k, xd]).astype(jnp.bfloat16)
        hops[k] = (
            copies.go(joined.at[k, beyond, 0], x_in.at[k, 0], {"x": east}),
            copies.go(joined.at[k, beyond, 1], x_in.at[k, 1], {"x": west}),
        )

    def last_hop(k):
        by_east, by_west = hops[k]
        by_east.wait_recv()
        x_sum[k, 0, 0] = add(joined[k, east, 0], x_in[k, 0]).astype(jnp.bfloat16)
        x_sum[k, 0, 1] = joined[k, east, 1]
        one = copies.go(x_sum.at[k, 0], x_in.at[k, pl.ds(2, 2)], {"x": east})
        by_west.wait_recv()
        x_sum[k, 1, 0] = joined[k, west, 0]
        x_sum[k, 1, 1] = add(joined[k, west, 1], x_in[k, 1]).astype(jnp.bfloat16)
        two = copies.go(x_sum.at[k, 1], x_in.at[k, pl.ds(4, 2)], {"x": west})
        lasts[k] = (one, two)

    away = 1 - zl

    def pair(k):
        one, two = lasts[k]
        one.wait_recv()
        two.wait_recv()
        z_out[k] = (
            add(joined[k, x, away], x_in[k, 2 + away])
            + x_in[k, 4 + away].astype(jnp.float32)
        ).astype(jnp.bfloat16)
        pairs[k] = copies.go(z_out.at[k], z_in.at[k], {"zl": away})

    def finish(k):
        pairs[k].wait_recv()
        total = (
            add(joined[k, x, zl], x_in[k, 2 + zl])
            + x_in[k, 4 + zl].astype(jnp.float32)
            + z_in[k].astype(jnp.float32)
        )
        tokens[y, z, c, pl.ds(k * 32, 32)] = (rest[k].astype(jnp.float32) + total).astype(
            jnp.bfloat16
        )

    class Wave:
        def __init__(self, wave):
            self.shared = []
            k_even, k_odd = 2 * wave, 2 * wave + 1

            def piece(feature, plane, k, part):
                if part is None:
                    return tokens.at[feature, plane, c, pl.ds(k * 32, 32)]
                return tokens.at[feature, plane, c, pl.ds(k * 32 + part * 16, 16)]

            def share(ref):
                self.shared.append(copies.go(ref, ref, {"c": other}))

            self.rows, self.columns = [], []

            def fan(plane, k):
                ref = piece(y, plane, k, None)
                return [copies.go(ref, ref, {"y": to}) for to in (right, left, far)]

            def start_row(plane):
                self.rows.append((fan(plane, k_even), plane))

            def start_column(feature):
                ring = Ring(
                    copies, z, 8, over, under,
                    lambda at, part: piece(feature, at, k_odd, part), lambda at: None,
                )
                self.columns.append((ring, feature))

            def turn_row(at):
                coming, plane = self.rows[at]
                for copy in coming:
                    copy.wait_recv()
                share(tokens.at[:, plane, c, pl.ds(k_even * 32, 32)])

            def turn_column(at):
                ring, feature = self.columns[at]
                ring.turn()
                if ring.step == 4:
                    share(tokens.at[feature, :, c, pl.ds(k_odd * 32, 32)])

            def begin():
                self.b = fan(z, k_odd)
                self.a = Ring(
                    copies, z, 8, over, under,
                    lambda at, part: piece(y, at, k_even, part), start_row,
                )
                start_column(y)
                start_row(z)

            def turn_b(at):
                self.b[at].wait_recv()
                start_column((left, right, far)[at])

            plan = [
                "b0", "b1", "a", "b2", "c0", "a", "r0", "c1", "c2", "c3", "a", "c0", "r1", "r2",
                "c1", "c2", "c3", "a", "c0", "r3", "r4", "c1", "c2", "c3", "r5", "r6", "c0",
                "r7", "c1", "c2", "c3",
            ]
            self.steps = [begin]
            for word in plan:
                if word == "a":
                    self.steps.append(lambda: self.a.turn())
                elif word[0] == "b":
                    self.steps.append(lambda at=int(word[1]): turn_b(at))
                elif word[0] == "c":
                    self.steps.append(lambda at=int(word[1]): turn_column(at))
                else:
                    self.steps.append(lambda at=int(word[1]): turn_row(at))

        def wait(self):
            for copy in self.shared:
                copy.wait_recv()

    lane = lax.broadcasted_iota(jnp.int32, (256, 512), 1)

    def multiply(wave, target):
        line, core = target // 2, lax.rem(target, 2)
        acc = jnp.zeros((256, 512), jnp.float32)
        squares = jnp.zeros((256, 128), jnp.float32)
        for feature in range(4):
            block = jnp.concatenate(
                [tokens[feature, 2 * a + line, core, pl.ds(wave * 64, 64)] for a in range(4)],
                axis=0,
            ).astype(jnp.float32)
            square = block * block
            squares += (square[:, :128] + square[:, 128:256]) + (
                square[:, 256:384] + square[:, 384:]
            )
            at = pl.ds(feature * 512, 512)
            scaled = (block * gain[:, at]).astype(jnp.bfloat16)
            acc += lax.dot_general(
                scaled, weight[:, at], nt, preferred_element_type=jnp.float32
            )
        squares = jnp.sum(squares, axis=1, keepdims=True)
        high = squares.astype(jnp.bfloat16).astype(jnp.float32)
        low = squares - high
        return jnp.where(lane == 224, high, jnp.where(lane == 225, low, acc))

    def narrow(value):
        return value.astype(jnp.bfloat16)

    class Sums:
        def __init__(self, wave):
            self.wave = wave
            self.steps = [self.send_far, self.send_east, self.send_west, self.keep, self.end]

        def send_far(self):
            w = self.wave
            product[w, 0] = narrow(multiply(w, beyond))
            self.half = (
                copies.go(product.at[w, 0, pl.ds(0, 128)], half_in.at[w, 0], {"x": east}),
                copies.go(product.at[w, 0, pl.ds(128, 128)], half_in.at[w, 1], {"x": west}),
            )

        def send_east(self):
            w = self.wave
            block = multiply(w, east)
            self.half[0].wait_recv()
            product[w, 1, pl.ds(0, 128)] = narrow(block[:128] + half_in[w, 0].astype(jnp.float32))
            product[w, 1, pl.ds(128, 128)] = narrow(block[128:])
            self.one = copies.go(product.at[w, 1], whole_in.at[w, 0], {"x": east})

        def send_west(self):
            w = self.wave
            block = multiply(w, west)
            self.half[1].wait_recv()
            product[w, 2, pl.ds(0, 128)] = narrow(block[:128])
            product[w, 2, pl.ds(128, 128)] = narrow(
                block[128:] + half_in[w, 1].astype(jnp.float32)
            )
            self.two = copies.go(product.at[w, 2], whole_in.at[w, 1], {"x": west})

        def keep(self):
            w = self.wave
            block = multiply(w, x)
            for a in range(4):
                summed[a, pl.ds(w * 64, 64)] = block[a * 64 : (a + 1) * 64]

        def end(self):
            w = self.wave
            self.one.wait_recv()
            self.two.wait_recv()
            block = add(whole_in[w, 0], whole_in[w, 1])
            for a in range(4):
                summed[a, pl.ds(w * 64, 64)] += block[a * 64 : (a + 1) * 64]

    for k in range(4):
        project(k)
        if k > 0:
            hop(k - 1)
        if k > 1:
            last_hop(k - 2)
    hop(3)
    pair(0)
    pair(1)
    last_hop(2)
    last_hop(3)
    finish(0)
    finish(1)
    first, second = Wave(0), Wave(1)
    steps = list(first.steps)
    late = [lambda: pair(2), lambda: pair(3), lambda: finish(2), lambda: finish(3)]
    for at, task in zip((3, 5, 7, 9), late):
        steps.insert(at, task)
    mixed, rest_steps = steps[:overlap_from], list(second.steps)
    for task in steps[overlap_from:]:
        mixed.append(task)
        mixed.append(rest_steps.pop(0))
    mixed.append(first.wait)
    for copy in loads:
        mixed.append(copy.wait)
    sums = Sums(0)
    chores = list(sums.steps)
    for at, task in enumerate(rest_steps):
        mixed.append(task)
        if at % 5 == 4 and chores:
            mixed.append(chores.pop(0))
    mixed += chores
    mixed.append(second.wait)
    mixed += Sums(1).steps
    for task in mixed:
        task()
    copies.finish()


overlap_from = 24
any_spec = pl.BlockSpec(memory_space=pl.ANY)
vmem_spec = pl.BlockSpec(memory_space=pltpu.VMEM)
bf16, f32 = jnp.bfloat16, jnp.float32
mib = 1024 * 1024


def whole(*arrays):
    return pl.pallas_call(
        whole_kernel,
        out_shape=jax.ShapeDtypeStruct((4, 128, 512), f32),
        in_specs=[any_spec] * 8 + [vmem_spec, any_spec, any_spec],
        out_specs=vmem_spec,
        scratch_shapes=[
            pltpu.VMEM((4, 2, 768, 128), bf16),
            pltpu.VMEM((4, 2, 768, 128), bf16),
            pltpu.VMEM((4, 128, 128), bf16),
            pltpu.VMEM((4, 128, 128), bf16),
            pltpu.VMEM((4, 2, 128, 256), bf16),
            pltpu.VMEM((4, 2, 8, 128), jnp.int32),
            pltpu.VMEM((4, 512, 128), f32),
            pltpu.VMEM((4, 512, 128), f32),
            pltpu.VMEM((4, 512, 128), f32),
            pltpu.VMEM((4, 2, 256, 128), bf16),
            pltpu.VMEM((4, 2, 8, 256), f32),
            pltpu.VMEM((8, 256, 128), bf16),
            pltpu.VMEM((8, 8, 256), f32),
            pltpu.VMEM((4, 128, 256), bf16),
            pltpu.VMEM((4, 256, 512), bf16),
            pltpu.VMEM((4, 32, 512), bf16),
            pltpu.VMEM((2, 4, 4, 2, 32, 512), bf16),
            pltpu.VMEM((4, 4, 2, 32, 512), bf16),
            pltpu.VMEM((4, 4, 2, 32, 512), bf16),
            pltpu.VMEM((4, 6, 32, 512), bf16),
            pltpu.VMEM((4, 2, 2, 32, 512), bf16),
            pltpu.VMEM((4, 32, 512), bf16),
            pltpu.VMEM((4, 32, 512), bf16),
            pltpu.VMEM((4, 8, 2, 128, 512), bf16),
            pltpu.VMEM((512, 2048), bf16),
            pltpu.VMEM((2, 3, 256, 512), bf16),
            pltpu.VMEM((2, 2, 128, 512), bf16),
            pltpu.VMEM((2, 2, 256, 512), bf16),
            pltpu.SemaphoreType.DMA((320,)),
            pltpu.SemaphoreType.DMA((320,)),
            pltpu.SemaphoreType.DMA((16,)),
        ],
        compiler_params=pltpu.CompilerParams(
            collective_id=1, has_side_effects=True, vmem_limit_bytes=56 * mib
        ),
        name="whole",
    )(*arrays)


def on_device(
    queries,
    new_keys,
    new_values,
    pool_keys,
    pool_values,
    block_counts,
    out_weight,
    residual,
    ffn_gain,
    gating_matrix,
    up_weight,
):
    x = lax.axis_index("x")
    gain = lax.dynamic_slice(ffn_gain, (x * 2048,), (2048,)).astype(f32).reshape(1, 2048)
    summed = whole(
        pool_keys.reshape(768, 128),
        pool_values.reshape(768, 128),
        new_keys,
        new_values,
        queries,
        jnp.broadcast_to(block_counts.reshape(1, 1), (8, 128)),
        out_weight,
        residual,
        gain,
        gating_matrix.T,
        up_weight.T,
    ).reshape(512, 512)
    squares = summed[:, 224] + summed[:, 225]
    inv_rms = lax.rsqrt(squares / 8192.0 + norm_eps)
    gate = summed[:, :224] * inv_rms[:, None]
    up = summed[:, 256:480] * inv_rms[:, None]
    return jax.nn.silu(gate) * up


def solution(mesh):
    fine = Mesh(mesh.devices.reshape(sizes), axes)
    seq, head, store = ("zh", "y"), "x", ("zl", "c")
    in_specs = (
        P(seq, head),
        P(seq, head),
        P(seq, head),
        P(seq + store, None, head),
        P(seq + store, None, head),
        P(seq + store),
        P((head,) + store, seq),
        P(seq, None),
        P(),
        P(head, seq + store),
        P(head, seq + store),
    )
    out_specs = P(head, seq + store)
    return jax.shard_map(
        on_device, mesh=fine, in_specs=in_specs, out_specs=out_specs, check_vma=False
    )
```

```python
import math

import jax
import jax.numpy as jnp
from jax import lax
from jax.experimental import pallas as pl
from jax.experimental.pallas import tpu as pltpu
from jax.sharding import Mesh, PartitionSpec as P

axes = ("zh", "y", "x", "zl", "c")
sizes = (4, 4, 4, 2, 2)
neg_large = -1e30
pos_large = 1e30
norm_eps = 1e-05
head_dim = 128
score_log2 = math.log2(math.e) / math.sqrt(head_dim)
MESH = pl.DeviceIdType.MESH
nt = (((1,), (1,)), ((), ()))


class Copies:
    def __init__(self, send, recv):
        self.send, self.recv, self.count, self.started = send, recv, 0, []

    def make(self, src, dst, where):
        at = self.count
        self.count += 1
        return pltpu.make_async_remote_copy(
            src_ref=src,
            dst_ref=dst,
            send_sem=self.send.at[at],
            recv_sem=self.recv.at[at],
            device_id=where,
            device_id_type=MESH,
        )

    def go(self, src, dst, where):
        copy = self.make(src, dst, where)
        copy.start()
        self.started.append(copy)
        return copy

    def finish(self):
        for copy in self.started:
            copy.wait_send()


class Locals:
    def __init__(self, sems):
        self.sems, self.count = sems, 0

    def go(self, src, dst):
        copy = pltpu.make_async_copy(src, dst, self.sems.at[self.count])
        self.count += 1
        copy.start()
        return copy


def position():
    return tuple(lax.axis_index(name) for name in axes)


def around(index, extent, step):
    return lax.rem(index + (step + extent), extent)


def greet(peers):
    barrier = pltpu.get_barrier_semaphore()
    for where in peers:
        pl.semaphore_signal(barrier, inc=1, device_id=where, device_id_type=MESH)
    pl.semaphore_wait(barrier, len(peers))


class Ring:
    def __init__(self, copies, index, extent, forward, backward, piece, arrived):
        self.copies, self.index, self.extent = copies, index, extent
        self.ways, self.piece, self.arrived = (forward, backward), piece, arrived
        self.pending = [self.move(index, way) for way in range(2)]
        self.step = 0

    def move(self, at, way, part=None):
        ref = self.piece(at, part)
        return self.copies.go(ref, ref, self.ways[way])

    def turn(self):
        self.step += 1
        step, last = self.step, self.extent // 2
        for way in range(2):
            self.pending[way].wait_recv()
            if step < last:
                at = around(self.index, self.extent, step if way else -step)
                part = way if step == last - 1 else None
                self.pending[way] = self.move(at, way, part)
                self.arrived(at)
        if step == last:
            self.arrived(around(self.index, self.extent, last))


def whole_kernel(
    keys, values, new_keys, new_values, queries, counts, out_weight, residual, gain, gating,
    up_weight, summed,
    keys_all, values_all, new_keys_all, new_values_all, queries_all, counts_all, top, total,
    weighted, parts, stats, parts_in, stats_in, context, project_weight, rest, partial, sibling,
    joined, x_in, x_sum, z_in, z_out, tokens, weight, product, half_in, whole_in,
    send, recv, local,
):
    zh, y, x, zl, c = position()
    other = 1 - c
    right, left, far = around(y, 4, 1), around(y, 4, -1), around(y, 4, 2)
    east, west, beyond = around(x, 4, 1), around(x, 4, -1), around(x, 4, 2)
    z = 2 * zh + zl
    above, below = around(z, 8, 1), around(z, 8, -1)
    over = {"zh": above // 2, "zl": lax.rem(above, 2)}
    under = {"zh": below // 2, "zl": lax.rem(below, 2)}
    column = []
    for step in (4, 3, 5, 2, 6, 1, 7):
        there = around(z, 8, step)
        column.append({"zh": there // 2, "zl": lax.rem(there, 2)})
    lane_peers = [{"y": around(y, 4, step), "c": core} for step in (1, 3, 2) for core in (c, other)]
    lane_peers.append({"c": other})
    greet(lane_peers + column + [{"x": east}, {"x": west}])
    copies, here = Copies(send, recv), Locals(local)

    up, down = around(zh, 4, 1), around(zh, 4, -1)
    half = keys.shape[0] // 2

    def first(src, dst):
        return copies.go(src, dst, {"y": right}), copies.go(src, dst, {"y": left})

    def head_pair(part):
        return queries.at[:, pl.ds(pl.multiple_of(part * 512 + c * 256, 256), 256)]

    fresh_in = []
    for src, out in ((new_keys, new_keys_all), (new_values, new_values_all)):
        for to in (far, right, left):
            fresh_in.append(copies.go(src, out.at[y], {"y": to}))
    across = {
        "k": copies.go(keys, keys_all.at[y, c], {"c": other}),
        "v": copies.go(values, values_all.at[y, c], {"c": other}),
    }
    ring_q = []
    for part in range(2):
        to = queries_all.at[zh, part]
        ring_q.append(
            (
                copies.go(head_pair(part), to, {"zh": up}),
                copies.go(head_pair(part), to, {"zh": down}),
            )
        )
    tallies = [copies.go(counts, counts_all.at[y, c], where) for where in lane_peers]
    ring_k = first(keys, keys_all.at[y, c])
    ring_v = first(values, values_all.at[y, c])
    own = [
        here.go(keys, keys_all.at[y, c]),
        here.go(values, values_all.at[y, c]),
        here.go(counts, counts_all.at[y, c]),
        here.go(head_pair(0), queries_all.at[zh, 0]),
        here.go(head_pair(1), queries_all.at[zh, 1]),
        here.go(new_keys, new_keys_all.at[y]),
        here.go(new_values, new_values_all.at[y]),
    ]
    group = pl.ds(pl.multiple_of((2 * zl + c) * 32, 32), 32)

    def tile(to):
        return residual.at[group, pl.ds(pl.multiple_of(x * 2048 + to * 512, 512), 512)]

    rest_in = [copies.go(tile(to), rest.at[y], {"y": to}) for to in (right, left, far)]
    own_late = [
        here.go(out_weight, project_weight.at[zh]),
        here.go(tile(y), rest.at[y]),
    ]
    loads = [
        here.go(gating, weight.at[pl.ds(0, 224)]),
        here.go(up_weight, weight.at[pl.ds(256, 224)]),
    ]
    weight[pl.ds(224, 32), :] = jnp.zeros((32, 2048), jnp.bfloat16)
    weight[pl.ds(480, 32), :] = jnp.zeros((32, 2048), jnp.bfloat16)

    def wide(value):
        return jnp.concatenate([value, value], axis=1)

    def meet(zq, part, holders, fresh=False, with_new=False):
        rows = jnp.concatenate(
            [queries_all[zq, part, :, pl.ds(0, 128)], queries_all[zq, part, :, pl.ds(128, 128)]],
            axis=0,
        )
        at = pl.ds(part * 256, 256)
        best, blocks = None, []
        for there, core in holders:
            scores = lax.dot_general(
                rows, keys_all[there, core], nt, preferred_element_type=jnp.float32
            )
            tally = counts_all[there, core]
            for slot in range(3):
                dead = jnp.where(tally > slot, -pos_large, pos_large).astype(jnp.float32)[:1]
                piece = scores[:, slot * 256 : (slot + 1) * 256]
                highest = jnp.minimum(jnp.maximum(piece[:, :128], piece[:, 128:]), -dead)
                best = highest if best is None else jnp.maximum(best, highest)
                blocks.append((piece, dead))
        if with_new:
            keys_now = jnp.concatenate(
                [new_keys_all[2 * zl], new_keys_all[2 * zl + 1]], axis=0
            )
            scores = lax.dot_general(rows, keys_now, nt, preferred_element_type=jnp.float32)
            key_token = (zh * 4 + 2 * zl) * 128 + lax.broadcasted_iota(jnp.int32, (256, 256), 1)
            query_token = (zq * 4 + y) * 128 + lax.rem(
                lax.broadcasted_iota(jnp.int32, (256, 256), 0), 128
            )
            scores = jnp.where(key_token <= query_token, scores, -pos_large)
            best = jnp.maximum(best, jnp.maximum(scores[:, :128], scores[:, 128:]))
            new_scores = jnp.where(key_token <= query_token, scores, -3.0 * pos_large)
        highest = jnp.max(best, axis=1, keepdims=True)
        if fresh:
            now = jnp.broadcast_to(highest, (256, 128))
        else:
            old = top[zq, at, :]
            now = jnp.maximum(old, highest)
            factor = jnp.exp2((old - now) * score_log2)
        top[zq, at, :] = now
        weights = [
            jnp.exp2((piece - wide(jnp.maximum(now, dead))) * score_log2) for piece, dead in blocks
        ]
        if with_new:
            weights.append(jnp.exp2((new_scores - wide(now)) * score_log2))
        sums = None
        for value in weights:
            added = value[:, :128] + value[:, 128:]
            sums = added if sums is None else sums + added
        if not fresh:
            sums = sums + total[zq, at, :] * factor
        total[zq, at, :] = sums
        acc = None if fresh else weighted[zq, at, :] * factor
        for number, (there, core) in enumerate(holders):
            three = jnp.concatenate(
                [value.astype(jnp.bfloat16) for value in weights[number * 3 : number * 3 + 3]],
                axis=1,
            )
            one = jnp.dot(three, values_all[there, core], preferred_element_type=jnp.float32)
            acc = one if acc is None else acc + one
        if with_new:
            values_now = jnp.concatenate(
                [new_values_all[2 * zl], new_values_all[2 * zl + 1]], axis=0
            )
            acc = acc + jnp.dot(
                weights[-1].astype(jnp.bfloat16), values_now, preferred_element_type=jnp.float32
            )
        weighted[zq, at, :] = acc

    both_own = [(y, c), (y, other)]
    both_sides = [(left, c), (right, c), (left, other), (right, other)]
    both_far = [(far, c), (far, other)]

    def near(zq):
        for part in range(2):
            meet(zq, part, both_own, fresh=True, with_new=True)

    def sides(zq):
        for part in range(2):
            meet(zq, part, both_sides)

    for copy in own:
        copy.wait()
    across["k"].wait_recv()
    across["v"].wait_recv()
    for copy in fresh_in + tallies[6:]:
        copy.wait_recv()
    near(zh)
    for pair_q in ring_q:
        for copy in pair_q:
            copy.wait_recv()
    far_q = [
        copies.go(queries_all.at[down, 0], queries_all.at[down, 0], {"zh": up}),
        copies.go(queries_all.at[up, 1], queries_all.at[up, 1], {"zh": down}),
    ]
    for copy in own_late:
        copy.wait()

    def weight_piece(at, part):
        if part is None:
            return project_weight.at[at]
        return project_weight.at[at, pl.ds(part * 128, 128)]

    ring_w = Ring(copies, zh, 4, {"zh": up}, {"zh": down}, weight_piece, lambda at: None)
    near(down)
    onward = []

    def pass_on(name, ring, out):
        ring[0].wait_recv()
        piece = out.at[left, c, pl.ds(0, half)]
        one = copies.go(piece, piece, {"y": right})
        across[name, 0] = copies.go(out.at[left, c], out.at[left, c], {"c": other})
        ring[1].wait_recv()
        piece = out.at[right, c, pl.ds(half, half)]
        two = copies.go(piece, piece, {"y": left})
        across[name, 1] = copies.go(out.at[right, c], out.at[right, c], {"c": other})
        onward.append((one, two, out))

    pass_on("k", ring_k, keys_all)
    near(up)
    pass_on("v", ring_v, values_all)
    for copy in far_q:
        copy.wait_recv()
    near(around(zh, 4, 2))
    for name in ("k", "v"):
        for side in range(2):
            across[name, side].wait_recv()
    for copy in tallies[:4]:
        copy.wait_recv()

    def turn(number, carry):
        sides(around(zh, 4, number))
        return carry

    lax.fori_loop(0, 2, turn, 0)
    for number, (one, two, out) in enumerate(onward):
        one.wait_recv()
        two.wait_recv()
        across["far", number] = copies.go(out.at[far, c], out.at[far, c], {"c": other})
    ring_w.turn()
    lax.fori_loop(2, 4, turn, 0)
    across["far", 0].wait_recv()
    across["far", 1].wait_recv()
    for copy in tallies[4:6]:
        copy.wait_recv()
    arriving = []
    for step in (2, 1, 3, 0):
        zq = around(zh, 4, step)
        for part in range(2):
            meet(zq, part, both_far)
            at = pl.ds(part * 256, 256)
            sums = jnp.broadcast_to(
                jnp.sum(total[zq, at, :], axis=1, keepdims=True), (256, 128)
            )
            parts[zq, part] = (weighted[zq, at, :] / jnp.where(sums > 0.0, sums, 1.0)).astype(
                jnp.bfloat16
            )
            lane = lax.broadcasted_iota(jnp.int32, (256, 128), 1)
            stats[zq, part] = jnp.transpose(jnp.where(lane < 4, top[zq, at, :], sums))[:8]
        for to in (zl, 1 - zl):
            if step == 0 and to is zl:
                continue
            where = {"zh": zq, "zl": to}
            arriving.append(copies.go(stats.at[zq, to], stats_in.at[z], where))
            arriving.append(copies.go(parts.at[zq, to], parts_in.at[z], where))
    stats_in[z] = stats[zh, zl]
    parts_in[z] = parts[zh, zl]
    ring_w.turn()
    for copy in arriving:
        copy.wait_recv()
    tops = jnp.concatenate([stats_in[i, pl.ds(0, 1), :] for i in range(8)], axis=0)
    sums = jnp.concatenate([stats_in[i, pl.ds(4, 1), :] for i in range(8)], axis=0)
    scales = jnp.exp2((tops - jnp.max(tops, axis=0, keepdims=True)) * score_log2) * sums
    scales = scales / jnp.sum(scales, axis=0, keepdims=True)
    scales = jnp.transpose(
        jnp.concatenate([scales, jnp.zeros((120, 256), jnp.float32)], axis=0)
    )
    for head in range(2):
        at = pl.ds(head * 128, 128)
        acc = jnp.zeros((128, 128), jnp.float32)
        for i in range(8):
            acc += parts_in[i, at, :].astype(jnp.float32) * scales[
                head * 128 : (head + 1) * 128, i : i + 1
            ]
        context[y, :, at] = acc.astype(jnp.bfloat16)

    context_in = [
        copies.go(context.at[y], context.at[y], {"y": to}) for to in (far, right, left)
    ]
    for copy in context_in:
        copy.wait_recv()
    for copy in rest_in:
        copy.wait_recv()

    def add(one, two):
        return one.astype(jnp.float32) + two.astype(jnp.float32)

    swaps, hops, lasts, pairs = {}, {}, {}, {}

    def project(k):
        for xd in range(4):
            block = jnp.dot(
                context[k], project_weight[xd], preferred_element_type=jnp.float32
            ).astype(jnp.bfloat16)
            for a in range(2):
                for b in range(2):
                    first = (2 * a + b) * 32
                    partial[b, k, xd, a] = block[first : first + 32]
        swaps[k] = copies.go(partial.at[other, k], sibling.at[k], {"c": other})

    def hop(k):
        swaps[k].wait_recv()
        for xd in (beyond, east, west, x):
            joined[k, xd] = add(partial[c, k, xd], sibling[k, xd]).astype(jnp.bfloat16)
        hops[k] = (
            copies.go(joined.at[k, beyond, 0], x_in.at[k, 0], {"x": east}),
            copies.go(joined.at[k, beyond, 1], x_in.at[k, 1], {"x": west}),
            copies.go(joined.at[k, east, 1], x_in.at[k, 3], {"x": east}),
            copies.go(joined.at[k, west, 0], x_in.at[k, 4], {"x": west}),
        )

    def last_hop(k):
        by_east, by_west, plain_east, plain_west = hops[k]
        by_east.wait_recv()
        x_sum[k, 0] = add(joined[k, east, 0], x_in[k, 0]).astype(jnp.bfloat16)
        one = copies.go(x_sum.at[k, 0], x_in.at[k, 2], {"x": east})
        by_west.wait_recv()
        x_sum[k, 1] = add(joined[k, west, 1], x_in[k, 1]).astype(jnp.bfloat16)
        two = copies.go(x_sum.at[k, 1], x_in.at[k, 5], {"x": west})
        lasts[k] = (plain_east, plain_west, one, two)

    away = 1 - zl

    def pair(k):
        for copy in lasts[k]:
            copy.wait_recv()
        z_out[k] = (
            add(joined[k, x, away], x_in[k, 2 + away])
            + x_in[k, 4 + away].astype(jnp.float32)
        ).astype(jnp.bfloat16)
        pairs[k] = copies.go(z_out.at[k], z_in.at[k], {"zl": away})

    def finish(k):
        pairs[k].wait_recv()
        total = (
            add(joined[k, x, zl], x_in[k, 2 + zl])
            + x_in[k, 4 + zl].astype(jnp.float32)
            + z_in[k].astype(jnp.float32)
        )
        tokens[y, z, c, pl.ds(k * 32, 32)] = (rest[k].astype(jnp.float32) + total).astype(
            jnp.bfloat16
        )

    class Wave:
        def __init__(self, wave):
            self.shared = []
            k_even, k_odd = 2 * wave, 2 * wave + 1

            def piece(feature, plane, k, part):
                if part is None:
                    return tokens.at[feature, plane, c, pl.ds(k * 32, 32)]
                return tokens.at[feature, plane, c, pl.ds(k * 32 + part * 16, 16)]

            def share(ref):
                self.shared.append(copies.go(ref, ref, {"c": other}))

            self.rows, self.columns = [], []

            def fan(plane, k):
                ref = piece(y, plane, k, None)
                return [copies.go(ref, ref, {"y": to}) for to in (right, left, far)]

            def start_row(plane):
                self.rows.append((fan(plane, k_even), plane))

            def start_column(feature):
                ring = Ring(
                    copies, z, 8, over, under,
                    lambda at, part: piece(feature, at, k_odd, part), lambda at: None,
                )
                self.columns.append((ring, feature))

            def turn_row(at):
                coming, plane = self.rows[at]
                for copy in coming:
                    copy.wait_recv()
                share(tokens.at[:, plane, c, pl.ds(k_even * 32, 32)])

            def turn_column(at):
                ring, feature = self.columns[at]
                ring.turn()
                if ring.step == 4:
                    share(tokens.at[feature, :, c, pl.ds(k_odd * 32, 32)])

            def begin():
                self.b = fan(z, k_odd)
                self.a = Ring(
                    copies, z, 8, over, under,
                    lambda at, part: piece(y, at, k_even, part), start_row,
                )
                start_column(y)
                start_row(z)

            def turn_b(at):
                self.b[at].wait_recv()
                start_column((left, right, far)[at])

            plan = [
                "b0", "b1", "a", "b2", "c0", "a", "r0", "c1", "c2", "c3", "a", "c0", "r1", "r2",
                "c1", "c2", "c3", "a", "c0", "r3", "r4", "c1", "c2", "c3", "r5", "r6", "c0",
                "r7", "c1", "c2", "c3",
            ]
            self.steps = [begin]
            for word in plan:
                if word == "a":
                    self.steps.append(lambda: self.a.turn())
                elif word[0] == "b":
                    self.steps.append(lambda at=int(word[1]): turn_b(at))
                elif word[0] == "c":
                    self.steps.append(lambda at=int(word[1]): turn_column(at))
                else:
                    self.steps.append(lambda at=int(word[1]): turn_row(at))

        def wait(self):
            for copy in self.shared:
                copy.wait_recv()

    lane = lax.broadcasted_iota(jnp.int32, (256, 512), 1)

    def multiply(wave, target):
        line, core = target // 2, lax.rem(target, 2)
        acc = jnp.zeros((256, 512), jnp.float32)
        squares = jnp.zeros((256, 128), jnp.float32)
        for feature in range(4):
            block = jnp.concatenate(
                [tokens[feature, 2 * a + line, core, pl.ds(wave * 64, 64)] for a in range(4)],
                axis=0,
            ).astype(jnp.float32)
            square = block * block
            squares += (square[:, :128] + square[:, 128:256]) + (
                square[:, 256:384] + square[:, 384:]
            )
            at = pl.ds(feature * 512, 512)
            scaled = (block * gain[:, at]).astype(jnp.bfloat16)
            acc += lax.dot_general(
                scaled, weight[:, at], nt, preferred_element_type=jnp.float32
            )
        squares = jnp.sum(squares, axis=1, keepdims=True)
        high = squares.astype(jnp.bfloat16).astype(jnp.float32)
        low = squares - high
        return jnp.where(lane == 224, high, jnp.where(lane == 225, low, acc))

    def narrow(value):
        return value.astype(jnp.bfloat16)

    class Sums:
        def __init__(self, wave):
            self.wave = wave
            self.steps = [
                self.send_far, self.send_east, self.send_west, self.add_far, self.keep, self.end
            ]

        def send_far(self):
            w = self.wave
            product[w, 0] = narrow(multiply(w, beyond))
            self.half = (
                copies.go(product.at[w, 0, pl.ds(0, 128)], half_in.at[w, 0], {"x": east}),
                copies.go(product.at[w, 0, pl.ds(128, 128)], half_in.at[w, 1], {"x": west}),
            )

        def send_east(self):
            w = self.wave
            block = multiply(w, east)
            product[w, 1, pl.ds(128, 128)] = narrow(block[128:])
            self.east_rows = block[:128]
            at = pl.ds(128, 128)
            self.last = [copies.go(product.at[w, 1, at], whole_in.at[w, 0, at], {"x": east})]

        def send_west(self):
            w = self.wave
            block = multiply(w, west)
            product[w, 2, pl.ds(0, 128)] = narrow(block[:128])
            self.west_rows = block[128:]
            at = pl.ds(0, 128)
            self.last.append(copies.go(product.at[w, 2, at], whole_in.at[w, 1, at], {"x": west}))

        def add_far(self):
            w = self.wave
            self.half[0].wait_recv()
            at = pl.ds(0, 128)
            product[w, 1, at] = narrow(self.east_rows + half_in[w, 0].astype(jnp.float32))
            self.last.append(copies.go(product.at[w, 1, at], whole_in.at[w, 0, at], {"x": east}))
            self.half[1].wait_recv()
            at = pl.ds(128, 128)
            product[w, 2, at] = narrow(self.west_rows + half_in[w, 1].astype(jnp.float32))
            self.last.append(copies.go(product.at[w, 2, at], whole_in.at[w, 1, at], {"x": west}))

        def keep(self):
            w = self.wave
            block = multiply(w, x)
            for a in range(4):
                summed[a, pl.ds(w * 64, 64)] = block[a * 64 : (a + 1) * 64]

        def end(self):
            w = self.wave
            for copy in self.last:
                copy.wait_recv()
            block = add(whole_in[w, 0], whole_in[w, 1])
            for a in range(4):
                summed[a, pl.ds(w * 64, 64)] += block[a * 64 : (a + 1) * 64]

    for k in range(4):
        project(k)
        if k > 0:
            hop(k - 1)
        if k > 1:
            last_hop(k - 2)
    hop(3)
    pair(0)
    pair(1)
    last_hop(2)
    last_hop(3)
    finish(0)
    finish(1)
    first, second = Wave(0), Wave(1)
    steps = list(first.steps)
    late = [lambda: pair(2), lambda: pair(3), lambda: finish(2), lambda: finish(3)]
    for at, task in zip((3, 5, 7, 9), late):
        steps.insert(at, task)
    mixed, rest_steps = steps[:overlap_from], list(second.steps)
    for task in steps[overlap_from:]:
        mixed.append(task)
        mixed.append(rest_steps.pop(0))
    mixed.append(first.wait)
    for copy in loads:
        mixed.append(copy.wait)
    sums = Sums(0)
    chores = list(sums.steps)
    for at, task in enumerate(rest_steps):
        mixed.append(task)
        if at % 4 == 3 and chores:
            mixed.append(chores.pop(0))
    mixed += chores
    mixed.append(second.wait)
    mixed += Sums(1).steps
    for task in mixed:
        task()
    copies.finish()


overlap_from = 24
any_spec = pl.BlockSpec(memory_space=pl.ANY)
vmem_spec = pl.BlockSpec(memory_space=pltpu.VMEM)
bf16, f32 = jnp.bfloat16, jnp.float32
mib = 1024 * 1024


def whole(*arrays):
    return pl.pallas_call(
        whole_kernel,
        out_shape=jax.ShapeDtypeStruct((4, 128, 512), f32),
        in_specs=[any_spec] * 8 + [vmem_spec, any_spec, any_spec],
        out_specs=vmem_spec,
        scratch_shapes=[
            pltpu.VMEM((4, 2, 768, 128), bf16),
            pltpu.VMEM((4, 2, 768, 128), bf16),
            pltpu.VMEM((4, 128, 128), bf16),
            pltpu.VMEM((4, 128, 128), bf16),
            pltpu.VMEM((4, 2, 128, 256), bf16),
            pltpu.VMEM((4, 2, 8, 128), jnp.int32),
            pltpu.VMEM((4, 512, 128), f32),
            pltpu.VMEM((4, 512, 128), f32),
            pltpu.VMEM((4, 512, 128), f32),
            pltpu.VMEM((4, 2, 256, 128), bf16),
            pltpu.VMEM((4, 2, 8, 256), f32),
            pltpu.VMEM((8, 256, 128), bf16),
            pltpu.VMEM((8, 8, 256), f32),
            pltpu.VMEM((4, 128, 256), bf16),
            pltpu.VMEM((4, 256, 512), bf16),
            pltpu.VMEM((4, 32, 512), bf16),
            pltpu.VMEM((2, 4, 4, 2, 32, 512), bf16),
            pltpu.VMEM((4, 4, 2, 32, 512), bf16),
            pltpu.VMEM((4, 4, 2, 32, 512), bf16),
            pltpu.VMEM((4, 6, 32, 512), bf16),
            pltpu.VMEM((4, 2, 32, 512), bf16),
            pltpu.VMEM((4, 32, 512), bf16),
            pltpu.VMEM((4, 32, 512), bf16),
            pltpu.VMEM((4, 8, 2, 128, 512), bf16),
            pltpu.VMEM((512, 2048), bf16),
            pltpu.VMEM((2, 3, 256, 512), bf16),
            pltpu.VMEM((2, 2, 128, 512), bf16),
            pltpu.VMEM((2, 2, 256, 512), bf16),
            pltpu.SemaphoreType.DMA((320,)),
            pltpu.SemaphoreType.DMA((320,)),
            pltpu.SemaphoreType.DMA((16,)),
        ],
        compiler_params=pltpu.CompilerParams(
            collective_id=1, has_side_effects=True, vmem_limit_bytes=56 * mib
        ),
        name="whole",
    )(*arrays)


def on_device(
    queries,
    new_keys,
    new_values,
    pool_keys,
    pool_values,
    block_counts,
    out_weight,
    residual,
    ffn_gain,
    gating_matrix,
    up_weight,
):
    x = lax.axis_index("x")
    gain = lax.dynamic_slice(ffn_gain, (x * 2048,), (2048,)).astype(f32).reshape(1, 2048)
    summed = whole(
        pool_keys.reshape(768, 128),
        pool_values.reshape(768, 128),
        new_keys,
        new_values,
        queries,
        jnp.broadcast_to(block_counts.reshape(1, 1), (8, 128)),
        out_weight,
        residual,
        gain,
        gating_matrix.T,
        up_weight.T,
    ).reshape(512, 512)
    squares = summed[:, 224] + summed[:, 225]
    inv_rms = lax.rsqrt(squares / 8192.0 + norm_eps)
    gate = summed[:, :224] * inv_rms[:, None]
    up = summed[:, 256:480] * inv_rms[:, None]
    return jax.nn.silu(gate) * up


def solution(mesh):
    fine = Mesh(mesh.devices.reshape(sizes), axes)
    seq, head, store = ("zh", "y"), "x", ("zl", "c")
    in_specs = (
        P(seq, head),
        P(seq, head),
        P(seq, head),
        P(seq + store, None, head),
        P(seq + store, None, head),
        P(seq + store),
        P((head,) + store, seq),
        P(seq, None),
        P(),
        P(head, seq + store),
        P(head, seq + store),
    )
    out_specs = P(head, seq + store)
    return jax.shard_map(
        on_device, mesh=fine, in_specs=in_specs, out_specs=out_specs, check_vma=False
    )
```
